128 devices in a mesh: row: 8 (over y, core), col: 16 (over z, x).
Axes of the slice: x: 4, y: 4, z: 4, core: 2. Of those that a mesh axis runs over, the one named last changes fastest.
Arguments:
- shell_velocity: bfloat16 [1024, 128, 128], P(('row', 'col')), may hold values from -6 to 6
- coupling: bfloat16 [1024, 2, 2, 256, 128], P(('row', 'col')), may hold values from -0.375 to 0.375
- coupling_dest: int32 [1024, 2], P(('row', 'col')), may hold values from 0 to 15, all different within a row; in each aligned block of 8 rows (0 to 7, 8 to 15, ...) at most 2 rows name the same one
- coupling_cluster: int32 [1024, 2], P(('row', 'col')), may hold values from 0 to 63
- near_blocks: bfloat16 [8, 16, 32, 2, 256, 256], P('row', 'col'), may hold values from -0.046875 to 0.046875
- far_v: bfloat16 [8, 16, 64, 2, 32, 256], P('row', 'col'), may hold values from -0.25 to 0.25
- far_u: bfloat16 [8, 16, 64, 2, 32, 256], P('row', 'col'), may hold values from -0.09375 to 0.09375
- block_pairs: int32 [8, 16, 96], P('row', 'col'), may hold values from 0 to 1023, as said below
Outputs:
- response: bfloat16 [32768, 128], P(('row', 'col'))
The draws below stay inside these ranges and needn't reach their ends.
Inputs may be any that keep to these rules, and one draw needn't show every extreme that they name: `coupling_dest`: the rows of one device name any column group at most 2 times, and some device names one exactly 2 times; the 2 entries of a row differ. `block_pairs`: each entry codes a row cluster r and column cluster c of its group as r * 64 + c; the entries of one group are distinct.
All inputs are finite; a program needn't handle non-finite values.
Results may differ from the reference program's by a relative error of at most 0.008.
Values may be sent and summed in bfloat16 or wider, within the bound.
No kernel may reach another device: no remote copies, remote signals or barrier semaphores. Data moves between devices by JAX's collectives and lax.ppermute only.
A program may use at most 128 MiB of HBM per device.

```python
import math
import jax
import jax.numpy as jnp
import numpy as np
from jax import lax

B = 256
RANK = 32
LOAD_CASES = 64
SB = 128
TOP = 2
RC_DEV = 16
CC_DEV = 64
NEAR_DEV = 32
FAR_DEV = 64
SHELL_DEV = 8
ROW_GROUPS = 8
COL_GROUPS = 16
MOST = 2
SHELLS = 1024
ROWS = 32768


def draw_block_pairs(key, part):
    keys = jax.random.split(jax.random.fold_in(key, 17), ROW_GROUPS * COL_GROUPS)

    def one_group(group_key):
        return jax.random.permutation(group_key, RC_DEV * CC_DEV)[:NEAR_DEV + FAR_DEV]
    values = jax.vmap(one_group)(keys)
    return values.reshape(ROW_GROUPS, COL_GROUPS, NEAR_DEV + FAR_DEV).astype(jnp.int32)


def with_ends(values, key, smallest, top_value):
    extent = values.shape
    place = [jax.random.randint(jax.random.fold_in(key, axis), (), 0, extent[axis]) for axis in range(len(extent))]
    values = values.at[tuple(place)].set(smallest)
    longest = extent.index(max(extent))
    place[longest] = (place[longest] + 1) % extent[longest]
    return values.at[tuple(place)].set(top_value)


def block_scale(rng, shape, cuts, smallest, high):
    loudness, own = 1.0, jax.random.fold_in(rng, 6)
    for dim, shards_of in cuts:
        draws = jnp.exp(jax.random.uniform(jax.random.fold_in(own, dim), (shards_of,), jnp.float32, smallest / len(cuts), high / len(cuts)))
        loudness = loudness * jnp.repeat(draws, shape[dim] // shards_of).reshape([-1 if axis == dim else 1 for axis in range(len(shape))])
    return loudness


def deal_out(key, own, number, rows, amount, top, bound, lean):
    sequence = jax.random.permutation(key, amount)
    packed, ordinary = portions_of(amount, rows * top, bound, lean, True), portions_of(amount, rows * top, bound, lean, False)
    places = jnp.arange(amount)

    def named(sizes, turn):
        used = int((sizes > 0).sum())
        fixed = max(1, used // 4)
        moved = fixed + (places - fixed + turn * (used - fixed)) % max(1, amount - fixed)
        return jnp.zeros((amount,), jnp.int32).at[sequence[jnp.where(places < fixed, places, moved)]].set(jnp.asarray(sizes, jnp.int32))

    sizes = jnp.where(number % 4 == 0, named(packed, number // 4), named(ordinary, number - number // 4 - 1))
    mixed = jax.random.permutation(jax.random.fold_in(own, 3), amount)
    source_of, sink = mixed[0:amount // 2 * 2:2], mixed[1:amount // 2 * 2:2]
    margin = jnp.minimum(sizes[source_of] - 1, bound - sizes[sink]) // 2
    margin = jnp.where((source_of == sequence[0]) | (sink == sequence[0]) | (sizes[sink] == 0), 0, jnp.maximum(margin, 0))
    moved = jax.random.randint(jax.random.fold_in(own, 4), (amount // 2,), 0, 1 << 20) % (margin + 1)
    sizes = sizes.at[source_of].add(-moved).at[sink].add(moved)
    members = jnp.searchsorted(jnp.cumsum(sizes), jnp.arange(rows * top), side="right").astype(jnp.int32)
    grid = members.reshape(top, rows).T
    grid = grid[jax.random.permutation(jax.random.fold_in(own, 1), rows)]
    turn = jax.random.randint(jax.random.fold_in(own, 2), (rows, 1), 0, top)
    return jnp.take_along_axis(grid, (jnp.arange(top)[None, :] + turn) % top, axis=1)


def portions_of(amount, total, limit, skew, full):
    loads = [(1 << 20) // math.isqrt(standing ** skew) + 1 for standing in range(1, amount + 1)]
    largest = limit if full else min(limit, max(-(-total // amount), total * loads[0] // sum(loads)))
    least = 1 if total - largest >= amount - 1 else 0
    counts, surplus = [largest] + [least] * (amount - 1), total - largest - least * (amount - 1)
    while surplus > 0:
        free = [i for i in range(1, amount) if counts[i] < largest] or [i for i in range(1, amount) if counts[i] < limit]
        pool, budget = sum([loads[i] for i in free]), surplus
        for i in free:
            addition = min(limit - counts[i], max(1, budget * loads[i] // pool), surplus)
            counts[i] = counts[i] + addition
            surplus = surplus - addition
    return np.array(counts)


def scatter_about(key, shape, deviation, limit, shards=(), kind=jnp.bfloat16):
    entries = deviation * jax.random.normal(key, shape, jnp.float32)
    if shards:
        entries = entries * block_scale(key, shape, shards, -0.22, 0.18)
    return jnp.clip(entries, -limit, limit).astype(kind)


def setup_inputs(seed: int = 0) -> dict:
    key_of = jax.random.split(jax.random.key(seed), 9)
    shell_velocity = scatter_about(key_of[0], (SHELLS, SB, 2 * LOAD_CASES), 1.0, 6.0, ((0, 128),))
    coupling = scatter_about(key_of[1], (SHELLS, TOP, 2, B, SB), (2 * SB) ** -0.5, 0.375, ((0, 128),))
    coupling_dest_keys = jax.random.split(jax.random.fold_in(key_of[2], 1), SHELLS // SHELL_DEV)
    coupling_dest_turns = jax.random.permutation(jax.random.fold_in(key_of[2], 3), SHELLS // SHELL_DEV)
    coupling_dest = jax.vmap(lambda own, number: deal_out(jax.random.fold_in(key_of[2], 2), own, number, SHELL_DEV, COL_GROUPS, TOP, MOST, 2))(coupling_dest_keys, coupling_dest_turns).reshape((SHELLS, TOP))
    coupling_cluster = with_ends(jax.random.randint(key_of[3], (SHELLS, TOP), 0, CC_DEV), jax.random.fold_in(key_of[3], 1), 0, CC_DEV - 1).astype(jnp.int32)
    near_blocks = scatter_about(key_of[4], (ROW_GROUPS, COL_GROUPS, NEAR_DEV, 2, B, B), (2 * B * COL_GROUPS * NEAR_DEV // RC_DEV) ** -0.5, 0.046875, ((0, 8), (1, 16)))
    far_v = scatter_about(key_of[5], (ROW_GROUPS, COL_GROUPS, FAR_DEV, 2, RANK, B), (2 * B) ** -0.5, 0.25, ((0, 8), (1, 16)))
    far_u = scatter_about(key_of[6], (ROW_GROUPS, COL_GROUPS, FAR_DEV, 2, RANK, B), (2 * RANK * COL_GROUPS * FAR_DEV // RC_DEV) ** -0.5, 0.09375, ((0, 8), (1, 16)))
    block_pairs = draw_block_pairs(jax.random.fold_in(key_of[8], 71), 0)
    return {"shell_velocity": shell_velocity, "coupling": coupling, "coupling_dest": coupling_dest, "coupling_cluster": coupling_cluster, "near_blocks": near_blocks, "far_v": far_v, "far_u": far_u, "block_pairs": block_pairs}


def rotate_blocks(values, load_count):
    return jnp.concatenate([-values[..., load_count:], values[..., :load_count]], axis=-1)


def reference(shell_velocity, coupling, coupling_dest, coupling_cluster, near_blocks, far_v, far_u, block_pairs):
    width = 2 * LOAD_CASES

    def shell_terms(inputs):
        coup, velo = inputs
        coup_f = coup.astype(jnp.float32)
        velo_f = velo.astype(jnp.float32)
        out = jnp.einsum('stpq,sqk->stpk', coup_f[:, :, 0], velo_f)
        out = out + jnp.einsum('stpq,sqk->stpk', coup_f[:, :, 1], rotate_blocks(velo_f, LOAD_CASES))
        return out.astype(jnp.bfloat16)

    groups = SHELLS // SHELL_DEV
    contributions = lax.map(shell_terms, (coupling.reshape(groups, SHELL_DEV, TOP, 2, B, SB),
                                          shell_velocity.reshape(groups, SHELL_DEV, SB, width)))
    contributions = lax.optimization_barrier(contributions.reshape(SHELLS * TOP, B, width))
    target = (coupling_dest * CC_DEV + coupling_cluster).reshape(-1).astype(jnp.int32)
    source_sum = jax.ops.segment_sum(contributions.astype(jnp.float32), target, num_segments=COL_GROUPS * CC_DEV)
    sources = source_sum.astype(jnp.bfloat16).reshape(COL_GROUPS, CC_DEV, B, width)

    def group_terms(inputs):
        near_group, right_group, left_group, pair_group, col_group = inputs
        local_src = lax.optimization_barrier(sources[col_group]).astype(jnp.float32)
        owners = (pair_group // CC_DEV).astype(jnp.int32)
        columns = (pair_group % CC_DEV).astype(jnp.int32)
        nearby_input = local_src[columns[:NEAR_DEV]]
        nearby_factor = near_group.astype(jnp.float32)
        nearby_contribution = jnp.einsum('dym,dmg->dyg', nearby_factor[:, 0], nearby_input)
        nearby_contribution = nearby_contribution + jnp.einsum('dym,dmg->dyg', nearby_factor[:, 1], rotate_blocks(nearby_input, LOAD_CASES))
        distant_input = local_src[columns[NEAR_DEV:]]
        right_factor_matrix = right_group.astype(jnp.float32)
        expansion_coefficients = jnp.einsum('dyz,dzi->dyi', right_factor_matrix[:, 0], distant_input)
        expansion_coefficients = expansion_coefficients + jnp.einsum('dyz,dzi->dyi', right_factor_matrix[:, 1], rotate_blocks(distant_input, LOAD_CASES))
        expansion_coefficients = lax.optimization_barrier(expansion_coefficients.astype(jnp.bfloat16)).astype(jnp.float32)
        left_f = left_group.astype(jnp.float32)
        far_term = jnp.einsum('brp,brk->bpk', left_f[:, 0], expansion_coefficients)
        far_term = far_term + jnp.einsum('brp,brk->bpk', left_f[:, 1], rotate_blocks(expansion_coefficients, LOAD_CASES))
        all_terms = jnp.concatenate([nearby_contribution, far_term], axis=0)
        return jax.ops.segment_sum(all_terms, owners, num_segments=RC_DEV)

    count = ROW_GROUPS * COL_GROUPS
    col_index = (jnp.arange(count) % COL_GROUPS).astype(jnp.int32)
    partials = lax.map(group_terms, (
        near_blocks.reshape(count, NEAR_DEV, 2, B, B),
        far_v.reshape(count, FAR_DEV, 2, RANK, B),
        far_u.reshape(count, FAR_DEV, 2, RANK, B),
        block_pairs.reshape(count, NEAR_DEV + FAR_DEV),
        col_index))
    partials = partials.reshape(ROW_GROUPS, COL_GROUPS, RC_DEV * B, width)
    response = jnp.sum(partials, axis=1).astype(jnp.bfloat16)
    return response.reshape(ROWS, width)
```

```python
import jax
import jax.numpy as jnp
from jax import lax
from jax.experimental import pallas as pl
from jax.experimental.pallas import tpu as pltpu
from jax.sharding import PartitionSpec as P

LOADS = 64
WIDTH = 128
PANELS = 256
SHELL_DEV = 8
TOP = 2
ROWS = 8
COLS = 16
CLUSTERS = 64
NEAR = 32
FAR = 64
SLOTS = 2
PIECE = WIDTH // ROWS
DATA = SLOTS * 2 * PIECE
MESSAGE = DATA + 8
NEAR_STEP = 4
FAR_STEP = 8
STEPS = NEAR // NEAR_STEP
VMEM_LIMIT = 40 * 1024 * 1024

F32 = jnp.float32
BF16 = jnp.bfloat16


def dot_t(a, b):
    return lax.dot_general(a, b, (((1,), (1,)), ((), ())), preferred_element_type=F32)


def dot_n(a, b):
    return lax.dot_general(a, b, (((1,), (0,)), ((), ())), preferred_element_type=F32)


def rotate_rows(values):
    half = values.shape[0] // 2
    return jnp.concatenate([-values[half:], values[:half]], axis=0)


def contribution_kernel(dest_ref, cluster_ref, velocity_ref, coupling_ref, out_ref, count_ref, ids_ref):
    step = pl.program_id(0)

    @pl.when(step == 0)
    def _():
        for h in range(COLS):
            count_ref[h] = 0
            ids_ref[2 * h] = CLUSTERS
            ids_ref[2 * h + 1] = CLUSTERS

    velocity = velocity_ref[0].astype(F32).T
    wide = jnp.concatenate([velocity, rotate_rows(velocity)], axis=1).astype(BF16)
    for t in range(TOP):
        h = dest_ref[step, t]
        slot = jnp.minimum(count_ref[h], SLOTS - 1)
        count_ref[h] = slot + 1
        ids_ref[2 * h + slot] = cluster_ref[step, t]
        blocks = jnp.concatenate([coupling_ref[0, t, 0], coupling_ref[0, t, 1]], axis=1)
        product = dot_t(wide, blocks).astype(BF16)
        start = pl.multiple_of(slot * (2 * PIECE), 2 * PIECE)
        for r in range(ROWS):
            for half in range(2):
                out_ref[r, h, pl.ds(start + half * PIECE, PIECE), :] = product[
                    r * PIECE : (r + 1) * PIECE, half * 128 : (half + 1) * 128
                ]

    @pl.when(step == SHELL_DEV - 1)
    def _():
        me = lax.axis_index("row") * COLS + lax.axis_index("col")
        row = lax.broadcasted_iota(jnp.int32, (8, 128), 0)
        lane = lax.broadcasted_iota(jnp.int32, (8, 128), 1)
        place = row * 128 + lane
        for h in range(COLS):
            tile = jnp.where(place == 2 * me, ids_ref[2 * h], 0)
            tile = jnp.where(place == 2 * me + 1, ids_ref[2 * h + 1], tile)
            tile = tile.astype(F32).astype(BF16)
            for r in range(ROWS):
                out_ref[r, h, DATA:MESSAGE, :] = tile


def contributions(dest, cluster, velocity, coupling):
    return pl.pallas_call(
        contribution_kernel,
        grid=(SHELL_DEV,),
        out_shape=jax.ShapeDtypeStruct((ROWS, COLS, MESSAGE, 128), BF16),
        in_specs=[
            pl.BlockSpec(memory_space=pltpu.SMEM),
            pl.BlockSpec(memory_space=pltpu.SMEM),
            pl.BlockSpec((1, 128, WIDTH), lambda s: (s, 0, 0)),
            pl.BlockSpec((1, TOP, 2, PANELS, 128), lambda s: (s, 0, 0, 0, 0)),
        ],
        out_specs=pl.BlockSpec((ROWS, COLS, MESSAGE, 128), lambda s: (0, 0, 0, 0)),
        scratch_shapes=[pltpu.SMEM((COLS,), jnp.int32), pltpu.SMEM((2 * COLS,), jnp.int32)],
        compiler_params=pltpu.CompilerParams(vmem_limit_bytes=VMEM_LIMIT),
        name="contributions",
    )(dest, cluster, velocity, coupling)


def cluster_kernel(got_ref, out_ref, total_ref, ids_vec_ref, ids_ref, sem):
    devices = got_ref.shape[0]
    ids = jnp.zeros((8, 128), F32)
    for s in range(devices):
        ids = ids + got_ref[s, DATA:MESSAGE, :].astype(F32)
    ids_vec_ref[...] = ids.astype(jnp.int32)
    copy = pltpu.make_async_copy(ids_vec_ref, ids_ref, sem)
    copy.start()
    total_ref[...] = jnp.zeros_like(total_ref)
    copy.wait()

    def add(s, carry):
        for slot in range(SLOTS):
            k = ids_ref[s // 64, 2 * (s % 64) + slot]
            piece = got_ref[s, slot * 2 * PIECE : (slot + 1) * 2 * PIECE, :]
            total_ref[k] = total_ref[k] + piece.astype(F32)
        return carry

    lax.fori_loop(0, devices, add, 0, unroll=8)
    out_ref[...] = total_ref[:CLUSTERS].astype(BF16)


def cluster_sums(got):
    return pl.pallas_call(
        cluster_kernel,
        out_shape=jax.ShapeDtypeStruct((CLUSTERS, 2 * PIECE, 128), BF16),
        in_specs=[pl.BlockSpec(memory_space=pltpu.VMEM)],
        out_specs=pl.BlockSpec(memory_space=pltpu.VMEM),
        scratch_shapes=[
            pltpu.VMEM((CLUSTERS + 1, 2 * PIECE, 128), F32),
            pltpu.VMEM((8, 128), jnp.int32),
            pltpu.SMEM((8, 128), jnp.int32),
            pltpu.SemaphoreType.DMA,
        ],
        compiler_params=pltpu.CompilerParams(vmem_limit_bytes=VMEM_LIMIT),
        name="cluster_sums",
    )(got)


def shift_rows(values, pairs):
    return lax.ppermute(values, "row", pairs)


def gather_pieces(own):
    half = CLUSTERS // 2
    up = [(s, (s + 2) % ROWS) for s in range(ROWS)]
    down = [(s, (s - 2) % ROWS) for s in range(ROWS)]
    twin = [(s, s ^ 1) for s in range(ROWS)]
    below = shift_rows(own, up)
    above = shift_rows(own, down)
    far_low = shift_rows(below[:half], up)
    far_high = shift_rows(above[half:], down)
    pieces = [(own, 0, 0), (below, 0, 3), (above, 0, 1), (far_low, 0, 2), (far_high, half, 2)]
    result = []
    for values, first, offset in pieces:
        result.append((values, first, offset, 0))
        result.append((shift_rows(values, twin), first, offset, 1))
    return result


def operator_kernel(places, pairs_ref, *refs):
    count = len(places)
    piece_refs = refs[:count]
    near_ref, right_ref, left_ref, out_ref, source_ref, total_ref, sem = refs[count:]
    step = pl.program_id(0)

    @pl.when(step == 0)
    def _():
        me = lax.axis_index("row")
        copies = []
        for i, (first, size, offset, core) in enumerate(places):
            row = ((me // 2 + offset) % 4) * 2 + (me + core) % 2
            start = pl.multiple_of(row * PIECE, PIECE)
            for part in range(2):
                copies.append(
                    pltpu.make_async_copy(
                        piece_refs[i].at[:, pl.ds(part * PIECE, PIECE), :],
                        source_ref.at[pl.ds(first, size), pl.ds(start, PIECE), pl.ds(part * 128, 128)],
                        sem.at[2 * i + part],
                    )
                )
        for copy in copies:
            copy.start()
        total_ref[...] = jnp.zeros_like(total_ref)
        for copy in copies:
            copy.wait()

    def sources(place):
        code = pairs_ref[place]
        values = source_ref[code % CLUSTERS]
        return code // CLUSTERS, jnp.concatenate([values, rotate_rows(values)], axis=1)

    for j in range(NEAR_STEP):
        owner, wide = sources(step * NEAR_STEP + j)
        blocks = jnp.concatenate([near_ref[j, 0], near_ref[j, 1]], axis=1)
        total_ref[owner] = total_ref[owner] + dot_t(wide, blocks)
    for j in range(FAR_STEP):
        owner, wide = sources(NEAR + step * FAR_STEP + j)
        right = jnp.concatenate([right_ref[j, 0], right_ref[j, 1]], axis=1)
        coeffs = dot_t(wide, right).astype(BF16)
        term = dot_n(coeffs, left_ref[j, 0]) + dot_n(rotate_rows(coeffs), left_ref[j, 1])
        total_ref[owner] = total_ref[owner] + term

    @pl.when(step == STEPS - 1)
    def _():
        out_ref[...] = total_ref[...].astype(BF16)


def apply_operator(pairs, pieces, near, right, left):
    places = [(first, values.shape[0], offset, core) for values, first, offset, core in pieces]

    def kernel(*refs):
        operator_kernel(places, *refs)

    return pl.pallas_call(
        kernel,
        grid=(STEPS,),
        out_shape=jax.ShapeDtypeStruct((COLS, WIDTH, PANELS), BF16),
        in_specs=[pl.BlockSpec(memory_space=pltpu.SMEM)]
        + [pl.BlockSpec(memory_space=pl.ANY)] * len(pieces)
        + [
            pl.BlockSpec((NEAR_STEP, 2, PANELS, PANELS), lambda s: (s, 0, 0, 0)),
            pl.BlockSpec((FAR_STEP, 2, 32, PANELS), lambda s: (s, 0, 0, 0)),
            pl.BlockSpec((FAR_STEP, 2, 32, PANELS), lambda s: (s, 0, 0, 0)),
        ],
        out_specs=pl.BlockSpec((COLS, WIDTH, PANELS), lambda s: (0, 0, 0)),
        scratch_shapes=[
            pltpu.VMEM((CLUSTERS, WIDTH, PANELS), BF16),
            pltpu.VMEM((COLS, WIDTH, PANELS), F32),
            pltpu.SemaphoreType.DMA((2 * len(pieces),)),
        ],
        compiler_params=pltpu.CompilerParams(vmem_limit_bytes=VMEM_LIMIT),
        name="operator",
    )(pairs, *[piece[0] for piece in pieces], near, right, left)


def response_kernel(got_ref, out_ref):
    total = got_ref[0].astype(F32)
    for i in range(1, COLS):
        total = total + got_ref[i].astype(F32)
    out_ref[...] = total.T.astype(BF16)


def response_sum(got):
    return pl.pallas_call(
        response_kernel,
        out_shape=jax.ShapeDtypeStruct((PANELS, WIDTH), BF16),
        in_specs=[pl.BlockSpec(memory_space=pltpu.VMEM)],
        out_specs=pl.BlockSpec(memory_space=pltpu.VMEM),
        compiler_params=pltpu.CompilerParams(vmem_limit_bytes=VMEM_LIMIT),
        name="response_sum",
    )(got)


def per_device(velocity, coupling, dest, cluster, near, far_v, far_u, pairs):
    messages = contributions(dest, cluster, velocity, coupling)
    messages = messages.reshape(ROWS * COLS, MESSAGE, 128)
    got = lax.all_to_all(messages, ("row", "col"), split_axis=0, concat_axis=0, tiled=True)
    own = cluster_sums(got)
    pieces = gather_pieces(own)
    partial = apply_operator(pairs.reshape(-1), pieces, near[0, 0], far_v[0, 0], far_u[0, 0])
    gathered = lax.all_to_all(partial, "col", split_axis=0, concat_axis=0, tiled=True)
    return response_sum(gathered)


def solution(mesh):
    return jax.shard_map(
        per_device,
        mesh=mesh,
        in_specs=(
            P(("row", "col"), None, None),
            P(("row", "col"), None, None, None, None),
            P(("row", "col"), None),
            P(("row", "col"), None),
            P("row", "col", None, None, None, None),
            P("row", "col", None, None, None, None),
            P("row", "col", None, None, None, None),
            P("row", "col", None),
        ),
        out_specs=P(("row", "col"), None),
        check_vma=False,
    )
```

```python
import jax
import jax.numpy as jnp
from jax import lax
from jax.experimental import pallas as pl
from jax.experimental.pallas import tpu as pltpu
from jax.sharding import PartitionSpec as P

LOADS = 64
WIDTH = 128
PANELS = 256
SHELL_DEV = 8
TOP = 2
ROWS = 8
COLS = 16
CLUSTERS = 64
NEAR = 32
FAR = 64
SLOTS = 2
PIECE = WIDTH // ROWS
DATA = SLOTS * 2 * PIECE
MESSAGE = DATA + 8
NEAR_STEP = 8
FAR_STEP = 16
RANK = 32
STEPS = NEAR // NEAR_STEP
VMEM_LIMIT = 12 * 1024 * 1024
FIRST_LIMIT = 54 * 1024 * 1024

F32 = jnp.float32
BF16 = jnp.bfloat16


def dot_t(a, b):
    return lax.dot_general(a, b, (((1,), (1,)), ((), ())), preferred_element_type=F32)


def dot_n(a, b):
    return lax.dot_general(a, b, (((1,), (0,)), ((), ())), preferred_element_type=F32)


def rotate_rows(values):
    half = values.shape[0] // 2
    return jnp.concatenate([-values[half:], values[:half]], axis=0)


def contribution_kernel(
    dest_ref, cluster_ref, velocity_hbm, coupling_hbm, out_ref, count_ref, ids_ref, velocity_ref, coupling_ref, sem
):
    velocity_copy = pltpu.make_async_copy(velocity_hbm, velocity_ref, sem.at[SHELL_DEV])
    copies = [
        pltpu.make_async_copy(coupling_hbm.at[s], coupling_ref.at[s], sem.at[s]) for s in range(SHELL_DEV)
    ]
    velocity_copy.start()
    for copy in copies:
        copy.start()
    for h in range(COLS):
        count_ref[h] = 0
        ids_ref[2 * h] = CLUSTERS
        ids_ref[2 * h + 1] = CLUSTERS
    velocity_copy.wait()
    for s in range(SHELL_DEV):
        velocity = velocity_ref[s].astype(F32).T
        wide = jnp.concatenate([velocity, rotate_rows(velocity)], axis=1).astype(BF16)
        copies[s].wait()
        for t in range(TOP):
            h = dest_ref[t, s]
            slot = jnp.minimum(count_ref[h], SLOTS - 1)
            count_ref[h] = slot + 1
            ids_ref[2 * h + slot] = cluster_ref[t, s]
            blocks = jnp.concatenate([coupling_ref[s, t, 0], coupling_ref[s, t, 1]], axis=1)
            product = dot_t(wide, blocks).astype(BF16)
            start = pl.multiple_of(slot * (2 * PIECE), 2 * PIECE)
            for r in range(ROWS):
                first = (r % 2) * LOADS + (r // 2) * PIECE
                for half in range(2):
                    out_ref[r, h, pl.ds(start + half * PIECE, PIECE), :] = product[
                        first : first + PIECE, half * 128 : (half + 1) * 128
                    ]
    me = lax.axis_index("row") * COLS + lax.axis_index("col")
    row = lax.broadcasted_iota(jnp.int32, (8, 128), 0)
    lane = lax.broadcasted_iota(jnp.int32, (8, 128), 1)
    place = row * 128 + lane
    for h in range(COLS):
        tile = jnp.where(place == 2 * me, ids_ref[2 * h], 0)
        tile = jnp.where(place == 2 * me + 1, ids_ref[2 * h + 1], tile)
        tile = tile.astype(F32).astype(BF16)
        for r in range(ROWS):
            out_ref[r, h, DATA:MESSAGE, :] = tile


def contributions(dest, cluster, velocity, coupling):
    return pl.pallas_call(
        contribution_kernel,
        out_shape=jax.ShapeDtypeStruct((ROWS, COLS, MESSAGE, 128), BF16),
        in_specs=[pl.BlockSpec(memory_space=pltpu.SMEM)] * 2 + [pl.BlockSpec(memory_space=pltpu.HBM)] * 2,
        out_specs=pl.BlockSpec(memory_space=pltpu.VMEM),
        scratch_shapes=[
            pltpu.SMEM((COLS,), jnp.int32),
            pltpu.SMEM((2 * COLS,), jnp.int32),
            pltpu.VMEM((SHELL_DEV, 128, WIDTH), BF16),
            pltpu.VMEM((SHELL_DEV, TOP, 2, PANELS, 128), BF16),
            pltpu.SemaphoreType.DMA((SHELL_DEV + 1,)),
        ],
        compiler_params=pltpu.CompilerParams(vmem_limit_bytes=FIRST_LIMIT),
        name="contributions",
    )(dest.T, cluster.T, velocity, coupling)


def cluster_kernel(got_ref, block_hbm, out_ref, block_ref, total_ref, ids_vec_ref, ids_ref, sem, block_sem):
    block_copy = pltpu.make_async_copy(block_hbm, block_ref, block_sem)
    block_copy.start()
    devices = got_ref.shape[0]
    ids = jnp.zeros((8, 128), F32)
    for s in range(devices):
        ids = ids + got_ref[s, DATA:MESSAGE, :].astype(F32)
    ids_vec_ref[...] = ids.astype(jnp.int32)
    copy = pltpu.make_async_copy(ids_vec_ref, ids_ref, sem)
    copy.start()
    total_ref[...] = jnp.zeros_like(total_ref)
    copy.wait()

    def add(s, carry):
        for slot in range(SLOTS):
            k = ids_ref[s // 64, 2 * (s % 64) + slot]
            piece = got_ref[s, slot * 2 * PIECE : (slot + 1) * 2 * PIECE, :]
            total_ref[k] = total_ref[k] + piece.astype(F32)
        return carry

    lax.fori_loop(0, devices, add, 0, unroll=8)
    out_ref[...] = total_ref[:CLUSTERS].astype(BF16)
    block_copy.wait()


def cluster_sums(got, blocks):
    return pl.pallas_call(
        cluster_kernel,
        out_shape=[
            jax.ShapeDtypeStruct((CLUSTERS, 2 * PIECE, 128), BF16),
            jax.ShapeDtypeStruct(blocks.shape, BF16),
        ],
        in_specs=[pl.BlockSpec(memory_space=pltpu.VMEM), pl.BlockSpec(memory_space=pltpu.HBM)],
        out_specs=[pl.BlockSpec(memory_space=pltpu.VMEM)] * 2,
        scratch_shapes=[
            pltpu.VMEM((CLUSTERS + 1, 2 * PIECE, 128), F32),
            pltpu.VMEM((8, 128), jnp.int32),
            pltpu.SMEM((8, 128), jnp.int32),
            pltpu.SemaphoreType.DMA,
            pltpu.SemaphoreType.DMA,
        ],
        compiler_params=pltpu.CompilerParams(vmem_limit_bytes=VMEM_LIMIT),
        name="cluster_sums",
    )(got, blocks)


def shift_rows(values, pairs):
    return lax.ppermute(values, "row", pairs)


def gather_pieces(own):
    along = [(s, (s + 2) % ROWS if s % 2 == 0 else (s - 2) % ROWS) for s in range(ROWS)]
    twin = [(s, s ^ 1) for s in range(ROWS)]
    near_same = shift_rows(own, along)
    other = shift_rows(own, twin)
    near_other = shift_rows(other, along)
    far_same = shift_rows(near_same, along)
    back_other = shift_rows(near_same, twin)
    back_same = shift_rows(near_other, twin)
    far_other = shift_rows(far_same, twin)
    return [own, near_same, far_same, back_same, other, near_other, far_other, back_other]


def operator_kernel(pairs_ref, *refs):
    piece_refs = refs[:ROWS]
    near_ref, right_ref, left_ref, out_ref, total_ref = refs[ROWS:]
    turn = jnp.where(lax.axis_index("row") % 2 == 0, -1.0, 1.0).astype(F32)

    def rotated(values):
        half = values.shape[0] // 2
        return jnp.concatenate([values[half:], -values[:half]], axis=0) * turn.astype(values.dtype)

    def sources(place):
        code = pairs_ref[place]
        column = code % CLUSTERS
        parts = [
            jnp.concatenate([ref[column, :PIECE], ref[column, PIECE:]], axis=1) for ref in piece_refs
        ]
        return code // CLUSTERS, jnp.concatenate(parts, axis=0)

    total_ref[...] = jnp.zeros_like(total_ref)

    def go(step, carry):
        for j in range(NEAR_STEP):
            owner, values = sources(step * NEAR_STEP + j)
            wide = jnp.concatenate([values, rotated(values)], axis=1)
            i = step * NEAR_STEP + j
            blocks = jnp.concatenate([near_ref[i, 0], near_ref[i, 1]], axis=1)
            total_ref[owner] = total_ref[owner] + dot_t(wide, blocks)
        owners, coeffs = [], []
        for j in range(FAR_STEP):
            owner, values = sources(NEAR + step * FAR_STEP + j)
            owners.append(owner)
            coeffs.append(dot_t(values, right_ref[step * FAR_STEP + j].reshape(2 * RANK, PANELS)))
        for j in range(FAR_STEP):
            value = (coeffs[j][:, :RANK] + rotated(coeffs[j][:, RANK:])).astype(BF16).astype(F32)
            coeffs[j] = jnp.concatenate([value, rotated(value)], axis=1).astype(BF16)
        for j in range(FAR_STEP):
            term = dot_n(coeffs[j], left_ref[step * FAR_STEP + j].reshape(2 * RANK, PANELS))
            total_ref[owners[j]] = total_ref[owners[j]] + term
        return carry

    lax.fori_loop(0, STEPS, go, 0)
    out_ref[...] = total_ref[...].astype(BF16)


def apply_operator(pairs, pieces, near, right, left):
    whole = pl.BlockSpec(memory_space=pltpu.VMEM)
    return pl.pallas_call(
        operator_kernel,
        out_shape=jax.ShapeDtypeStruct((COLS, WIDTH, PANELS), BF16),
        in_specs=[pl.BlockSpec(memory_space=pltpu.SMEM)] + [whole] * (len(pieces) + 3),
        out_specs=whole,
        scratch_shapes=[pltpu.VMEM((COLS, WIDTH, PANELS), F32)],
        compiler_params=pltpu.CompilerParams(vmem_limit_bytes=VMEM_LIMIT),
        name="operator",
    )(pairs, *pieces, near, right, left)


def response_kernel(got_ref, out_ref, rows_ref):
    total = got_ref[0].astype(F32)
    for i in range(1, COLS):
        total = total + got_ref[i].astype(F32)
    me = lax.axis_index("row")
    y, core = me // 2, me % 2
    ahead = jnp.where(core == 0, 3, 1)
    for part in range(2):
        base = jnp.where(part == 0, core, 1 - core) * LOADS
        for i, offset in enumerate((0, ahead, 2, 4 - ahead)):
            start = pl.multiple_of(base + ((y + offset) % 4) * PIECE, PIECE)
            first = part * LOADS + i * PIECE
            rows_ref[pl.ds(start, PIECE), :] = total[first : first + PIECE]
    out_ref[...] = rows_ref[...].T.astype(BF16)


def response_sum(got):
    return pl.pallas_call(
        response_kernel,
        out_shape=jax.ShapeDtypeStruct((PANELS, WIDTH), BF16),
        in_specs=[pl.BlockSpec(memory_space=pltpu.VMEM)],
        out_specs=pl.BlockSpec(memory_space=pltpu.VMEM),
        scratch_shapes=[pltpu.VMEM((WIDTH, PANELS), F32)],
        compiler_params=pltpu.CompilerParams(vmem_limit_bytes=VMEM_LIMIT),
        name="response_sum",
    )(got)


def per_device(velocity, coupling, dest, cluster, near, far_v, far_u, pairs):
    messages = contributions(dest, cluster, velocity, coupling)
    messages = messages.reshape(ROWS * COLS, MESSAGE, 128)
    got = lax.all_to_all(messages, ("row", "col"), split_axis=0, concat_axis=0, tiled=True)
    own, left = cluster_sums(got, far_u[0, 0])
    pieces = gather_pieces(own)
    partial = apply_operator(pairs.reshape(-1), pieces, near[0, 0], far_v[0, 0], left)
    gathered = lax.all_to_all(partial, "col", split_axis=0, concat_axis=0, tiled=True)
    return response_sum(gathered)


def solution(mesh):
    return jax.shard_map(
        per_device,
        mesh=mesh,
        in_specs=(
            P(("row", "col"), None, None),
            P(("row", "col"), None, None, None, None),
            P(("row", "col"), None),
            P(("row", "col"), None),
            P("row", "col", None, None, None, None),
            P("row", "col", None, None, None, None),
            P("row", "col", None, None, None, None),
            P("row", "col", None),
        ),
        out_specs=P(("row", "col"), None),
        check_vma=False,
    )
```

```python
import jax
import jax.numpy as jnp
from jax import lax
from jax.experimental import pallas as pl
from jax.experimental.pallas import tpu as pltpu
from jax.sharding import PartitionSpec as P

LOADS = 64
WIDTH = 128
PANELS = 256
SHELL_DEV = 8
TOP = 2
ROWS = 8
COLS = 16
CLUSTERS = 64
NEAR = 32
FAR = 64
SLOTS = 2
PIECE = WIDTH // ROWS
DATA = SLOTS * 2 * PIECE
MESSAGE = DATA + 8
NEAR_STEP = 16
FAR_STEP = 32
RANK = 32
STEPS = NEAR // NEAR_STEP
VMEM_LIMIT = 12 * 1024 * 1024
FIRST_LIMIT = 54 * 1024 * 1024

F32 = jnp.float32
BF16 = jnp.bfloat16


def dot_t(a, b):
    return lax.dot_general(a, b, (((1,), (1,)), ((), ())), preferred_element_type=F32)


def dot_n(a, b):
    return lax.dot_general(a, b, (((1,), (0,)), ((), ())), preferred_element_type=F32)


def rotate_rows(values):
    half = values.shape[0] // 2
    return jnp.concatenate([-values[half:], values[:half]], axis=0)


def contribution_kernel(
    dest_hbm,
    cluster_hbm,
    velocity_hbm,
    coupling_hbm,
    out_ref,
    dest_ref,
    cluster_ref,
    count_ref,
    ids_ref,
    velocity_ref,
    coupling_ref,
    sem,
):
    dest_copy = pltpu.make_async_copy(dest_hbm, dest_ref, sem.at[SHELL_DEV + 1])
    cluster_copy = pltpu.make_async_copy(cluster_hbm, cluster_ref, sem.at[SHELL_DEV + 2])
    velocity_copy = pltpu.make_async_copy(velocity_hbm, velocity_ref, sem.at[SHELL_DEV])
    copies = [
        pltpu.make_async_copy(coupling_hbm.at[s], coupling_ref.at[s], sem.at[s]) for s in range(SHELL_DEV)
    ]
    velocity_copy.start()
    copies[0].start()
    dest_copy.start()
    cluster_copy.start()
    for copy in copies[1:]:
        copy.start()
    for h in range(COLS):
        count_ref[h] = 0
        ids_ref[2 * h] = CLUSTERS
        ids_ref[2 * h + 1] = CLUSTERS
    velocity_copy.wait()
    for s in range(SHELL_DEV):
        velocity = velocity_ref[s].astype(F32).T
        wide = jnp.concatenate([velocity, rotate_rows(velocity)], axis=1).astype(BF16)
        copies[s].wait()
        if s == 0:
            dest_copy.wait()
            cluster_copy.wait()
        for t in range(TOP):
            h = dest_ref[t, s]
            slot = jnp.minimum(count_ref[h], SLOTS - 1)
            count_ref[h] = slot + 1
            ids_ref[2 * h + slot] = cluster_ref[t, s]
            blocks = jnp.concatenate([coupling_ref[s, t, 0], coupling_ref[s, t, 1]], axis=1)
            product = dot_t(wide, blocks).astype(BF16)
            start = pl.multiple_of(slot * (2 * PIECE), 2 * PIECE)
            for r in range(ROWS):
                first = (r % 2) * LOADS + (r // 2) * PIECE
                for half in range(2):
                    out_ref[r, h, pl.ds(start + half * PIECE, PIECE), :] = product[
                        first : first + PIECE, half * 128 : (half + 1) * 128
                    ]
    me = lax.axis_index("row") * COLS + lax.axis_index("col")
    row = lax.broadcasted_iota(jnp.int32, (8, 128), 0)
    lane = lax.broadcasted_iota(jnp.int32, (8, 128), 1)
    place = row * 128 + lane
    for h in range(COLS):
        tile = jnp.where(place == 2 * me, ids_ref[2 * h], 0)
        tile = jnp.where(place == 2 * me + 1, ids_ref[2 * h + 1], tile)
        tile = tile.astype(F32).astype(BF16)
        for r in range(ROWS):
            out_ref[r, h, DATA:MESSAGE, :] = tile


def contributions(dest, cluster, velocity, coupling):
    return pl.pallas_call(
        contribution_kernel,
        out_shape=jax.ShapeDtypeStruct((ROWS, COLS, MESSAGE, 128), BF16),
        in_specs=[pl.BlockSpec(memory_space=pltpu.HBM)] * 4,
        out_specs=pl.BlockSpec(memory_space=pltpu.VMEM),
        scratch_shapes=[
            pltpu.SMEM((TOP, SHELL_DEV), jnp.int32),
            pltpu.SMEM((TOP, SHELL_DEV), jnp.int32),
            pltpu.SMEM((COLS,), jnp.int32),
            pltpu.SMEM((2 * COLS,), jnp.int32),
            pltpu.VMEM((SHELL_DEV, 128, WIDTH), BF16),
            pltpu.VMEM((SHELL_DEV, TOP, 2, PANELS, 128), BF16),
            pltpu.SemaphoreType.DMA((SHELL_DEV + 3,)),
        ],
        compiler_params=pltpu.CompilerParams(vmem_limit_bytes=FIRST_LIMIT),
        name="contributions",
    )(dest.T, cluster.T, velocity, coupling)


def cluster_kernel(got_ref, block_hbm, out_ref, block_ref, total_ref, ids_vec_ref, ids_ref, sem, block_sem):
    block_copy = pltpu.make_async_copy(block_hbm, block_ref, block_sem)
    block_copy.start()
    devices = got_ref.shape[0]
    ids = jnp.zeros((8, 128), F32)
    for s in range(devices):
        ids = ids + got_ref[s, DATA:MESSAGE, :].astype(F32)
    ids_vec_ref[...] = ids.astype(jnp.int32)
    copy = pltpu.make_async_copy(ids_vec_ref, ids_ref, sem)
    copy.start()
    total_ref[...] = jnp.zeros_like(total_ref)
    copy.wait()

    def add(s, carry):
        for slot in range(SLOTS):
            k = ids_ref[s // 64, 2 * (s % 64) + slot]
            piece = got_ref[s, slot * 2 * PIECE : (slot + 1) * 2 * PIECE, :]
            total_ref[k] = total_ref[k] + piece.astype(F32)
        return carry

    lax.fori_loop(0, devices, add, 0, unroll=8)
    out_ref[...] = total_ref[:CLUSTERS].astype(BF16)
    block_copy.wait()


def cluster_sums(got, blocks):
    return pl.pallas_call(
        cluster_kernel,
        out_shape=[
            jax.ShapeDtypeStruct((CLUSTERS, 2 * PIECE, 128), BF16),
            jax.ShapeDtypeStruct(blocks.shape, BF16),
        ],
        in_specs=[pl.BlockSpec(memory_space=pltpu.VMEM), pl.BlockSpec(memory_space=pltpu.HBM)],
        out_specs=[pl.BlockSpec(memory_space=pltpu.VMEM)] * 2,
        scratch_shapes=[
            pltpu.VMEM((CLUSTERS + 1, 2 * PIECE, 128), F32),
            pltpu.VMEM((8, 128), jnp.int32),
            pltpu.SMEM((8, 128), jnp.int32),
            pltpu.SemaphoreType.DMA,
            pltpu.SemaphoreType.DMA,
        ],
        compiler_params=pltpu.CompilerParams(vmem_limit_bytes=VMEM_LIMIT),
        name="cluster_sums",
    )(got, blocks)


def shift_rows(values, pairs):
    return lax.ppermute(values, "row", pairs)


def gather_pieces(own):
    along = [(s, (s + 2) % ROWS if s % 2 == 0 else (s - 2) % ROWS) for s in range(ROWS)]
    twin = [(s, s ^ 1) for s in range(ROWS)]
    near_same = shift_rows(own, along)
    other = shift_rows(own, twin)
    near_other = shift_rows(other, along)
    far_same = shift_rows(near_same, along)
    back_other = shift_rows(near_same, twin)
    back_same = shift_rows(near_other, twin)
    far_other = shift_rows(far_same, twin)
    return [own, near_same, far_same, back_same, other, near_other, far_other, back_other]


def operator_kernel(pairs_ref, *refs):
    piece_refs = refs[:ROWS]
    near_ref, right_ref, left_ref, out_ref, total_ref = refs[ROWS:]
    turn = jnp.where(lax.axis_index("row") % 2 == 0, -1.0, 1.0).astype(F32)

    def rotated(values):
        half = values.shape[0] // 2
        return jnp.concatenate([values[half:], -values[:half]], axis=0) * turn.astype(values.dtype)

    def sources(place):
        code = pairs_ref[place]
        column = code % CLUSTERS
        parts = [
            jnp.concatenate([ref[column, :PIECE], ref[column, PIECE:]], axis=1) for ref in piece_refs
        ]
        return code // CLUSTERS, jnp.concatenate(parts, axis=0)

    total_ref[...] = jnp.zeros_like(total_ref)

    def go(step, carry):
        for j in range(NEAR_STEP):
            owner, values = sources(step * NEAR_STEP + j)
            wide = jnp.concatenate([values, rotated(values)], axis=1)
            i = step * NEAR_STEP + j
            blocks = jnp.concatenate([near_ref[i, 0], near_ref[i, 1]], axis=1)
            total_ref[owner] = total_ref[owner] + dot_t(wide, blocks)
        owners, coeffs = [], []
        for j in range(FAR_STEP):
            owner, values = sources(NEAR + step * FAR_STEP + j)
            owners.append(owner)
            coeffs.append(dot_t(values, right_ref[step * FAR_STEP + j].reshape(2 * RANK, PANELS)))
        for j in range(FAR_STEP):
            value = (coeffs[j][:, :RANK] + rotated(coeffs[j][:, RANK:])).astype(BF16).astype(F32)
            coeffs[j] = jnp.concatenate([value, rotated(value)], axis=1).astype(BF16)
        for j in range(FAR_STEP):
            term = dot_n(coeffs[j], left_ref[step * FAR_STEP + j].reshape(2 * RANK, PANELS))
            total_ref[owners[j]] = total_ref[owners[j]] + term
        return carry

    lax.fori_loop(0, STEPS, go, 0)
    out_ref[...] = total_ref[...].astype(BF16)


def apply_operator(pairs, pieces, near, right, left):
    whole = pl.BlockSpec(memory_space=pltpu.VMEM)
    return pl.pallas_call(
        operator_kernel,
        out_shape=jax.ShapeDtypeStruct((COLS, WIDTH, PANELS), BF16),
        in_specs=[pl.BlockSpec(memory_space=pltpu.SMEM)] + [whole] * (len(pieces) + 3),
        out_specs=whole,
        scratch_shapes=[pltpu.VMEM((COLS, WIDTH, PANELS), F32)],
        compiler_params=pltpu.CompilerParams(vmem_limit_bytes=VMEM_LIMIT),
        name="operator",
    )(pairs, *pieces, near, right, left)


def response_kernel(got_ref, out_ref, rows_ref):
    total = got_ref[0].astype(F32)
    for i in range(1, COLS):
        total = total + got_ref[i].astype(F32)
    me = lax.axis_index("row")
    y, core = me // 2, me % 2
    ahead = jnp.where(core == 0, 3, 1)
    for part in range(2):
        base = jnp.where(part == 0, core, 1 - core) * LOADS
        for i, offset in enumerate((0, ahead, 2, 4 - ahead)):
            start = pl.multiple_of(base + ((y + offset) % 4) * PIECE, PIECE)
            first = part * LOADS + i * PIECE
            rows_ref[pl.ds(start, PIECE), :] = total[first : first + PIECE]
    out_ref[...] = rows_ref[...].T.astype(BF16)


def response_sum(got):
    return pl.pallas_call(
        response_kernel,
        out_shape=jax.ShapeDtypeStruct((PANELS, WIDTH), BF16),
        in_specs=[pl.BlockSpec(memory_space=pltpu.VMEM)],
        out_specs=pl.BlockSpec(memory_space=pltpu.VMEM),
        scratch_shapes=[pltpu.VMEM((WIDTH, PANELS), F32)],
        compiler_params=pltpu.CompilerParams(vmem_limit_bytes=VMEM_LIMIT),
        name="response_sum",
    )(got)


def per_device(velocity, coupling, dest, cluster, near, far_v, far_u, pairs):
    messages = contributions(dest, cluster, velocity, coupling)
    messages = messages.reshape(ROWS * COLS, MESSAGE, 128)
    got = lax.all_to_all(messages, ("row", "col"), split_axis=0, concat_axis=0, tiled=True)
    own, left = cluster_sums(got, far_u[0, 0])
    pieces = gather_pieces(own)
    partial = apply_operator(pairs.reshape(-1), pieces, near[0, 0], far_v[0, 0], left)
    gathered = lax.all_to_all(partial, "col", split_axis=0, concat_axis=0, tiled=True)
    return response_sum(gathered)


def solution(mesh):
    return jax.shard_map(
        per_device,
        mesh=mesh,
        in_specs=(
            P(("row", "col"), None, None),
            P(("row", "col"), None, None, None, None),
            P(("row", "col"), None),
            P(("row", "col"), None),
            P("row", "col", None, None, None, None),
            P("row", "col", None, None, None, None),
            P("row", "col", None, None, None, None),
            P("row", "col", None),
        ),
        out_specs=P(("row", "col"), None),
        check_vma=False,
    )
```

```python
import jax
import jax.numpy as jnp
from jax import lax
from jax.experimental import pallas as pl
from jax.experimental.pallas import tpu as pltpu
from jax.sharding import PartitionSpec as P

LOADS = 64
WIDTH = 128
PANELS = 256
SHELL_DEV = 8
TOP = 2
ROWS = 8
COLS = 16
CLUSTERS = 64
NEAR = 32
FAR = 64
SLOTS = 2
PIECE = WIDTH // ROWS
DATA = SLOTS * 2 * PIECE
MESSAGE = DATA + 8
NEAR_STEP = 16
FAR_STEP = 32
RANK = 32
STEPS = NEAR // NEAR_STEP
VMEM_LIMIT = 12 * 1024 * 1024
FIRST_LIMIT = 54 * 1024 * 1024

F32 = jnp.float32
BF16 = jnp.bfloat16


def dot_t(a, b):
    return lax.dot_general(a, b, (((1,), (1,)), ((), ())), preferred_element_type=F32)


def dot_n(a, b):
    return lax.dot_general(a, b, (((1,), (0,)), ((), ())), preferred_element_type=F32)


def rotate_rows(values):
    half = values.shape[0] // 2
    return jnp.concatenate([-values[half:], values[:half]], axis=0)


def contribution_kernel(
    dest_hbm,
    cluster_hbm,
    velocity_hbm,
    coupling_hbm,
    out_ref,
    dest_ref,
    cluster_ref,
    count_ref,
    ids_ref,
    velocity_ref,
    coupling_ref,
    sem,
):
    dest_copy = pltpu.make_async_copy(dest_hbm, dest_ref, sem.at[SHELL_DEV + 1])
    cluster_copy = pltpu.make_async_copy(cluster_hbm, cluster_ref, sem.at[SHELL_DEV + 2])
    velocity_copy = pltpu.make_async_copy(velocity_hbm, velocity_ref, sem.at[SHELL_DEV])
    copies = [
        pltpu.make_async_copy(coupling_hbm.at[s], coupling_ref.at[s], sem.at[s]) for s in range(SHELL_DEV)
    ]
    velocity_copy.start()
    copies[0].start()
    dest_copy.start()
    cluster_copy.start()
    for copy in copies[1:]:
        copy.start()
    for h in range(COLS):
        count_ref[h] = 0
        ids_ref[2 * h] = CLUSTERS
        ids_ref[2 * h + 1] = CLUSTERS
    velocity_copy.wait()
    for s in range(SHELL_DEV):
        velocity = velocity_ref[s].T
        wide = jnp.concatenate([velocity, rotate_rows(velocity)], axis=1)
        copies[s].wait()
        if s == 0:
            dest_copy.wait()
            cluster_copy.wait()
        for t in range(TOP):
            h = dest_ref[t, s]
            slot = jnp.minimum(count_ref[h], SLOTS - 1)
            count_ref[h] = slot + 1
            ids_ref[2 * h + slot] = cluster_ref[t, s]
            blocks = jnp.concatenate([coupling_ref[s, t, 0], coupling_ref[s, t, 1]], axis=1)
            product = dot_t(wide, blocks).astype(BF16)
            start = pl.multiple_of(slot * (2 * PIECE), 2 * PIECE)
            for r in range(ROWS):
                first = (r % 2) * LOADS + (r // 2) * PIECE
                for half in range(2):
                    out_ref[r, h, pl.ds(start + half * PIECE, PIECE), :] = product[
                        first : first + PIECE, half * 128 : (half + 1) * 128
                    ]
    me = lax.axis_index("row") * COLS + lax.axis_index("col")
    row = lax.broadcasted_iota(jnp.int32, (8, 128), 0)
    lane = lax.broadcasted_iota(jnp.int32, (8, 128), 1)
    place = row * 128 + lane
    for h in range(COLS):
        tile = jnp.where(place == 2 * me, ids_ref[2 * h], 0)
        tile = jnp.where(place == 2 * me + 1, ids_ref[2 * h + 1], tile)
        tile = tile.astype(F32).astype(BF16)
        for r in range(ROWS):
            out_ref[r, h, DATA:MESSAGE, :] = tile


def contributions(dest, cluster, velocity, coupling):
    return pl.pallas_call(
        contribution_kernel,
        out_shape=jax.ShapeDtypeStruct((ROWS, COLS, MESSAGE, 128), BF16),
        in_specs=[pl.BlockSpec(memory_space=pltpu.HBM)] * 4,
        out_specs=pl.BlockSpec(memory_space=pltpu.VMEM),
        scratch_shapes=[
            pltpu.SMEM((TOP, SHELL_DEV), jnp.int32),
            pltpu.SMEM((TOP, SHELL_DEV), jnp.int32),
            pltpu.SMEM((COLS,), jnp.int32),
            pltpu.SMEM((2 * COLS,), jnp.int32),
            pltpu.VMEM((SHELL_DEV, 128, WIDTH), BF16),
            pltpu.VMEM((SHELL_DEV, TOP, 2, PANELS, 128), BF16),
            pltpu.SemaphoreType.DMA((SHELL_DEV + 3,)),
        ],
        compiler_params=pltpu.CompilerParams(vmem_limit_bytes=FIRST_LIMIT),
        name="contributions",
    )(dest.T, cluster.T, velocity, coupling)


def cluster_kernel(got_ref, block_hbm, out_ref, block_ref, total_ref, other_ref, ids_vec_ref, ids_ref, sem, block_sem):
    block_copy = pltpu.make_async_copy(block_hbm, block_ref, block_sem)
    block_copy.start()
    devices = got_ref.shape[0]
    ids = jnp.zeros((8, 128), F32)
    for s in range(devices):
        ids = ids + got_ref[s, DATA:MESSAGE, :].astype(F32)
    ids_vec_ref[...] = ids.astype(jnp.int32)
    copy = pltpu.make_async_copy(ids_vec_ref, ids_ref, sem)
    copy.start()
    total_ref[...] = jnp.zeros_like(total_ref)
    other_ref[...] = jnp.zeros_like(other_ref)
    copy.wait()

    for row in range(devices // 64):

        def add(i, carry):
            for slot, sums_ref in enumerate((total_ref, other_ref)):
                k = ids_ref[row, 2 * i + slot]
                piece = got_ref[row * 64 + i, slot * 2 * PIECE : (slot + 1) * 2 * PIECE, :]
                sums_ref[k] = sums_ref[k] + piece.astype(F32)
            return carry

        lax.fori_loop(0, 64, add, 0, unroll=8)
    out_ref[...] = (total_ref[:CLUSTERS] + other_ref[:CLUSTERS]).astype(BF16)
    block_copy.wait()


def cluster_sums(got, blocks):
    return pl.pallas_call(
        cluster_kernel,
        out_shape=[
            jax.ShapeDtypeStruct((CLUSTERS, 2 * PIECE, 128), BF16),
            jax.ShapeDtypeStruct(blocks.shape, BF16),
        ],
        in_specs=[pl.BlockSpec(memory_space=pltpu.VMEM), pl.BlockSpec(memory_space=pltpu.HBM)],
        out_specs=[pl.BlockSpec(memory_space=pltpu.VMEM)] * 2,
        scratch_shapes=[
            pltpu.VMEM((CLUSTERS + 1, 2 * PIECE, 128), F32),
            pltpu.VMEM((CLUSTERS + 1, 2 * PIECE, 128), F32),
            pltpu.VMEM((8, 128), jnp.int32),
            pltpu.SMEM((8, 128), jnp.int32),
            pltpu.SemaphoreType.DMA,
            pltpu.SemaphoreType.DMA,
        ],
        compiler_params=pltpu.CompilerParams(vmem_limit_bytes=VMEM_LIMIT),
        name="cluster_sums",
    )(got, blocks)


def shift_rows(values, pairs):
    return lax.ppermute(values, "row", pairs)


def gather_pieces(own):
    along = [(s, (s + 2) % ROWS if s % 2 == 0 else (s - 2) % ROWS) for s in range(ROWS)]
    twin = [(s, s ^ 1) for s in range(ROWS)]
    near_same = shift_rows(own, along)
    other = shift_rows(own, twin)
    near_other = shift_rows(other, along)
    far_same = shift_rows(near_same, along)
    back_other = shift_rows(near_same, twin)
    back_same = shift_rows(near_other, twin)
    far_other = shift_rows(far_same, twin)
    return [own, near_same, far_same, back_same, other, near_other, far_other, back_other]


def operator_kernel(pairs_ref, *refs):
    piece_refs = refs[:ROWS]
    near_ref, right_ref, left_ref, out_ref, total_ref = refs[ROWS:]
    turn = jnp.where(lax.axis_index("row") % 2 == 0, -1.0, 1.0).astype(F32)

    def rotated(values):
        half = values.shape[0] // 2
        return jnp.concatenate([values[half:], -values[:half]], axis=0) * turn.astype(values.dtype)

    def sources(place):
        code = pairs_ref[place]
        column = code % CLUSTERS
        parts = [
            jnp.concatenate([ref[column, :PIECE], ref[column, PIECE:]], axis=1) for ref in piece_refs
        ]
        return code // CLUSTERS, jnp.concatenate(parts, axis=0)

    total_ref[...] = jnp.zeros_like(total_ref)

    def go(step, carry):
        for j in range(NEAR_STEP):
            owner, values = sources(step * NEAR_STEP + j)
            wide = jnp.concatenate([values, rotated(values)], axis=1)
            i = step * NEAR_STEP + j
            blocks = jnp.concatenate([near_ref[i, 0], near_ref[i, 1]], axis=1)
            total_ref[owner] = total_ref[owner] + dot_t(wide, blocks)
        owners, coeffs = [], []
        for j in range(FAR_STEP):
            owner, values = sources(NEAR + step * FAR_STEP + j)
            owners.append(owner)
            coeffs.append(dot_t(values, right_ref[step * FAR_STEP + j].reshape(2 * RANK, PANELS)))
        for j in range(FAR_STEP):
            value = (coeffs[j][:, :RANK] + rotated(coeffs[j][:, RANK:])).astype(BF16)
            coeffs[j] = jnp.concatenate([value, rotated(value)], axis=1)
        for j in range(FAR_STEP):
            term = dot_n(coeffs[j], left_ref[step * FAR_STEP + j].reshape(2 * RANK, PANELS))
            total_ref[owners[j]] = total_ref[owners[j]] + term
        return carry

    lax.fori_loop(0, STEPS, go, 0)
    out_ref[...] = total_ref[...].astype(BF16)


def apply_operator(pairs, pieces, near, right, left):
    whole = pl.BlockSpec(memory_space=pltpu.VMEM)
    return pl.pallas_call(
        operator_kernel,
        out_shape=jax.ShapeDtypeStruct((COLS, WIDTH, PANELS), BF16),
        in_specs=[pl.BlockSpec(memory_space=pltpu.SMEM)] + [whole] * (len(pieces) + 3),
        out_specs=whole,
        scratch_shapes=[pltpu.VMEM((COLS, WIDTH, PANELS), F32)],
        compiler_params=pltpu.CompilerParams(vmem_limit_bytes=VMEM_LIMIT),
        name="operator",
    )(pairs, *pieces, near, right, left)


def response_kernel(got_ref, out_ref, rows_ref):
    total = got_ref[0].astype(F32)
    for i in range(1, COLS):
        total = total + got_ref[i].astype(F32)
    me = lax.axis_index("row")
    y, core = me // 2, me % 2
    ahead = jnp.where(core == 0, 3, 1)
    for part in range(2):
        base = jnp.where(part == 0, core, 1 - core) * LOADS
        for i, offset in enumerate((0, ahead, 2, 4 - ahead)):
            start = pl.multiple_of(base + ((y + offset) % 4) * PIECE, PIECE)
            first = part * LOADS + i * PIECE
            rows_ref[pl.ds(start, PIECE), :] = total[first : first + PIECE]
    out_ref[...] = rows_ref[...].T.astype(BF16)


def response_sum(got):
    return pl.pallas_call(
        response_kernel,
        out_shape=jax.ShapeDtypeStruct((PANELS, WIDTH), BF16),
        in_specs=[pl.BlockSpec(memory_space=pltpu.VMEM)],
        out_specs=pl.BlockSpec(memory_space=pltpu.VMEM),
        scratch_shapes=[pltpu.VMEM((WIDTH, PANELS), F32)],
        compiler_params=pltpu.CompilerParams(vmem_limit_bytes=VMEM_LIMIT),
        name="response_sum",
    )(got)


def per_device(velocity, coupling, dest, cluster, near, far_v, far_u, pairs):
    messages = contributions(dest, cluster, velocity, coupling)
    messages = messages.reshape(ROWS * COLS, MESSAGE, 128)
    got = lax.all_to_all(messages, ("row", "col"), split_axis=0, concat_axis=0, tiled=True)
    own, left = cluster_sums(got, far_u[0, 0])
    pieces = gather_pieces(own)
    partial = apply_operator(pairs.reshape(-1), pieces, near[0, 0], far_v[0, 0], left)
    gathered = lax.all_to_all(partial, "col", split_axis=0, concat_axis=0, tiled=True)
    return response_sum(gathered)


def solution(mesh):
    return jax.shard_map(
        per_device,
        mesh=mesh,
        in_specs=(
            P(("row", "col"), None, None),
            P(("row", "col"), None, None, None, None),
            P(("row", "col"), None),
            P(("row", "col"), None),
            P("row", "col", None, None, None, None),
            P("row", "col", None, None, None, None),
            P("row", "col", None, None, None, None),
            P("row", "col", None),
        ),
        out_specs=P(("row", "col"), None),
        check_vma=False,
    )
```

```python
import jax
import jax.numpy as jnp
from jax import lax
from jax.experimental import pallas as pl
from jax.experimental.pallas import tpu as pltpu
from jax.sharding import PartitionSpec as P

LOADS = 64
WIDTH = 128
PANELS = 256
SHELL_DEV = 8
TOP = 2
ROWS = 8
COLS = 16
CLUSTERS = 64
NEAR = 32
FAR = 64
SLOTS = 2
PIECE = WIDTH // ROWS
DATA = SLOTS * 2 * PIECE
MESSAGE = DATA + 8
NEAR_STEP = 16
FAR_STEP = 32
RANK = 32
STEPS = NEAR // NEAR_STEP
VMEM_LIMIT = 12 * 1024 * 1024
FIRST_LIMIT = 54 * 1024 * 1024

F32 = jnp.float32
BF16 = jnp.bfloat16


def dot_t(a, b):
    return lax.dot_general(a, b, (((1,), (1,)), ((), ())), preferred_element_type=F32)


def dot_n(a, b):
    return lax.dot_general(a, b, (((1,), (0,)), ((), ())), preferred_element_type=F32)


def rotate_rows(values):
    half = values.shape[0] // 2
    return jnp.concatenate([-values[half:], values[:half]], axis=0)


def contribution_kernel(
    dest_hbm,
    cluster_hbm,
    velocity_hbm,
    coupling_hbm,
    out_ref,
    dest_ref,
    cluster_ref,
    count_ref,
    ids_ref,
    velocity_ref,
    coupling_ref,
    sem,
):
    dest_copy = pltpu.make_async_copy(dest_hbm, dest_ref, sem.at[SHELL_DEV + 1])
    cluster_copy = pltpu.make_async_copy(cluster_hbm, cluster_ref, sem.at[SHELL_DEV + 2])
    velocity_copy = pltpu.make_async_copy(velocity_hbm, velocity_ref, sem.at[SHELL_DEV])
    copies = [
        pltpu.make_async_copy(coupling_hbm.at[s], coupling_ref.at[s], sem.at[s]) for s in range(SHELL_DEV)
    ]
    velocity_copy.start()
    copies[0].start()
    dest_copy.start()
    cluster_copy.start()
    for copy in copies[1:]:
        copy.start()
    for h in range(COLS):
        count_ref[h] = 0
        ids_ref[2 * h] = CLUSTERS
        ids_ref[2 * h + 1] = CLUSTERS
    velocity_copy.wait()
    for s in range(SHELL_DEV):
        velocity = velocity_ref[s].T
        wide = jnp.concatenate([velocity, rotate_rows(velocity)], axis=1)
        copies[s].wait()
        if s == 0:
            dest_copy.wait()
            cluster_copy.wait()
        for t in range(TOP):
            h = dest_ref[t, s]
            slot = jnp.minimum(count_ref[h], SLOTS - 1)
            count_ref[h] = slot + 1
            ids_ref[2 * h + slot] = cluster_ref[t, s]
            blocks = jnp.concatenate([coupling_ref[s, t, 0], coupling_ref[s, t, 1]], axis=1)
            product = dot_t(wide, blocks).astype(BF16)
            start = pl.multiple_of(slot * (2 * PIECE), 2 * PIECE)
            for r in range(ROWS):
                first = (r % 2) * LOADS + (r // 2) * PIECE
                for half in range(2):
                    out_ref[r, h, pl.ds(start + half * PIECE, PIECE), :] = product[
                        first : first + PIECE, half * 128 : (half + 1) * 128
                    ]
    me = lax.axis_index("row") * COLS + lax.axis_index("col")
    row = lax.broadcasted_iota(jnp.int32, (8, 128), 0)
    lane = lax.broadcasted_iota(jnp.int32, (8, 128), 1)
    place = row * 128 + lane
    for h in range(COLS):
        tile = jnp.where(place == 2 * me, ids_ref[2 * h], 0)
        tile = jnp.where(place == 2 * me + 1, ids_ref[2 * h + 1], tile)
        tile = tile.astype(F32).astype(BF16)
        for r in range(ROWS):
            out_ref[r, h, DATA:MESSAGE, :] = tile


def contributions(dest, cluster, velocity, coupling):
    return pl.pallas_call(
        contribution_kernel,
        out_shape=jax.ShapeDtypeStruct((ROWS, COLS, MESSAGE, 128), BF16),
        in_specs=[pl.BlockSpec(memory_space=pltpu.HBM)] * 4,
        out_specs=pl.BlockSpec(memory_space=pltpu.VMEM),
        scratch_shapes=[
            pltpu.SMEM((TOP, SHELL_DEV), jnp.int32),
            pltpu.SMEM((TOP, SHELL_DEV), jnp.int32),
            pltpu.SMEM((COLS,), jnp.int32),
            pltpu.SMEM((2 * COLS,), jnp.int32),
            pltpu.VMEM((SHELL_DEV, 128, WIDTH), BF16),
            pltpu.VMEM((SHELL_DEV, TOP, 2, PANELS, 128), BF16),
            pltpu.SemaphoreType.DMA((SHELL_DEV + 3,)),
        ],
        compiler_params=pltpu.CompilerParams(vmem_limit_bytes=FIRST_LIMIT),
        name="contributions",
    )(dest.T, cluster.T, velocity, coupling)


def cluster_kernel(got_ref, block_hbm, out_ref, block_ref, *refs):
    totals, (ids_vec_ref, ids_ref, sem, block_sem) = refs[:4], refs[4:]
    block_copy = pltpu.make_async_copy(block_hbm, block_ref, block_sem)
    block_copy.start()
    devices = got_ref.shape[0]
    ids = jnp.zeros((8, 128), F32)
    for s in range(devices):
        ids = ids + got_ref[s, DATA:MESSAGE, :].astype(F32)
    ids_vec_ref[...] = ids.astype(jnp.int32)
    copy = pltpu.make_async_copy(ids_vec_ref, ids_ref, sem)
    copy.start()
    for sums_ref in totals:
        sums_ref[...] = jnp.zeros_like(sums_ref)
    copy.wait()

    def add(i, carry):
        for j, sums_ref in enumerate(totals):
            row, slot = j // SLOTS, j % SLOTS
            k = ids_ref[row, 2 * i + slot]
            piece = got_ref[row * 64 + i, slot * 2 * PIECE : (slot + 1) * 2 * PIECE, :]
            sums_ref[k] = sums_ref[k] + piece.astype(F32)
        return carry

    lax.fori_loop(0, 64, add, 0, unroll=4)
    sums = [sums_ref[:CLUSTERS] for sums_ref in totals]
    out_ref[...] = ((sums[0] + sums[1]) + (sums[2] + sums[3])).astype(BF16)
    block_copy.wait()


def cluster_sums(got, blocks):
    return pl.pallas_call(
        cluster_kernel,
        out_shape=[
            jax.ShapeDtypeStruct((CLUSTERS, 2 * PIECE, 128), BF16),
            jax.ShapeDtypeStruct(blocks.shape, BF16),
        ],
        in_specs=[pl.BlockSpec(memory_space=pltpu.VMEM), pl.BlockSpec(memory_space=pltpu.HBM)],
        out_specs=[pl.BlockSpec(memory_space=pltpu.VMEM)] * 2,
        scratch_shapes=[
            pltpu.VMEM((CLUSTERS + 1, 2 * PIECE, 128), F32),
            pltpu.VMEM((CLUSTERS + 1, 2 * PIECE, 128), F32),
            pltpu.VMEM((CLUSTERS + 1, 2 * PIECE, 128), F32),
            pltpu.VMEM((CLUSTERS + 1, 2 * PIECE, 128), F32),
            pltpu.VMEM((8, 128), jnp.int32),
            pltpu.SMEM((8, 128), jnp.int32),
            pltpu.SemaphoreType.DMA,
            pltpu.SemaphoreType.DMA,
        ],
        compiler_params=pltpu.CompilerParams(vmem_limit_bytes=VMEM_LIMIT),
        name="cluster_sums",
    )(got, blocks)


def shift_rows(values, pairs):
    return lax.ppermute(values, "row", pairs)


def gather_pieces(own):
    along = [(s, (s + 2) % ROWS if s % 2 == 0 else (s - 2) % ROWS) for s in range(ROWS)]
    twin = [(s, s ^ 1) for s in range(ROWS)]
    near_same = shift_rows(own, along)
    other = shift_rows(own, twin)
    near_other = shift_rows(other, along)
    far_same = shift_rows(near_same, along)
    back_other = shift_rows(near_same, twin)
    back_same = shift_rows(near_other, twin)
    far_other = shift_rows(far_same, twin)
    return [own, near_same, far_same, back_same, other, near_other, far_other, back_other]


def operator_kernel(pairs_ref, *refs):
    piece_refs = refs[:ROWS]
    near_ref, right_ref, left_ref, out_ref, total_ref = refs[ROWS:]
    turn = jnp.where(lax.axis_index("row") % 2 == 0, -1.0, 1.0).astype(F32)

    def rotated(values):
        half = values.shape[0] // 2
        return jnp.concatenate([values[half:], -values[:half]], axis=0) * turn.astype(values.dtype)

    def sources(place):
        code = pairs_ref[place]
        column = code % CLUSTERS
        parts = [
            jnp.concatenate([ref[column, :PIECE], ref[column, PIECE:]], axis=1) for ref in piece_refs
        ]
        return code // CLUSTERS, jnp.concatenate(parts, axis=0)

    total_ref[...] = jnp.zeros_like(total_ref)

    def go(step, carry):
        for j in range(NEAR_STEP):
            owner, values = sources(step * NEAR_STEP + j)
            wide = jnp.concatenate([values, rotated(values)], axis=1)
            i = step * NEAR_STEP + j
            blocks = jnp.concatenate([near_ref[i, 0], near_ref[i, 1]], axis=1)
            total_ref[owner] = total_ref[owner] + dot_t(wide, blocks)
        owners, coeffs = [], []
        for j in range(FAR_STEP):
            owner, values = sources(NEAR + step * FAR_STEP + j)
            owners.append(owner)
            coeffs.append(dot_t(values, right_ref[step * FAR_STEP + j].reshape(2 * RANK, PANELS)))
        for j in range(FAR_STEP):
            value = (coeffs[j][:, :RANK] + rotated(coeffs[j][:, RANK:])).astype(BF16)
            coeffs[j] = jnp.concatenate([value, rotated(value)], axis=1)
        for j in range(FAR_STEP):
            term = dot_n(coeffs[j], left_ref[step * FAR_STEP + j].reshape(2 * RANK, PANELS))
            total_ref[owners[j]] = total_ref[owners[j]] + term
        return carry

    lax.fori_loop(0, STEPS, go, 0)
    out_ref[...] = total_ref[...].astype(BF16)


def apply_operator(pairs, pieces, near, right, left):
    whole = pl.BlockSpec(memory_space=pltpu.VMEM)
    return pl.pallas_call(
        operator_kernel,
        out_shape=jax.ShapeDtypeStruct((COLS, WIDTH, PANELS), BF16),
        in_specs=[pl.BlockSpec(memory_space=pltpu.SMEM)] + [whole] * (len(pieces) + 3),
        out_specs=whole,
        scratch_shapes=[pltpu.VMEM((COLS, WIDTH, PANELS), F32)],
        compiler_params=pltpu.CompilerParams(vmem_limit_bytes=VMEM_LIMIT),
        name="operator",
    )(pairs, *pieces, near, right, left)


def response_kernel(got_ref, out_ref, rows_ref):
    total = got_ref[0].astype(F32)
    for i in range(1, COLS):
        total = total + got_ref[i].astype(F32)
    me = lax.axis_index("row")
    y, core = me // 2, me % 2
    ahead = jnp.where(core == 0, 3, 1)
    for part in range(2):
        base = jnp.where(part == 0, core, 1 - core) * LOADS
        for i, offset in enumerate((0, ahead, 2, 4 - ahead)):
            start = pl.multiple_of(base + ((y + offset) % 4) * PIECE, PIECE)
            first = part * LOADS + i * PIECE
            rows_ref[pl.ds(start, PIECE), :] = total[first : first + PIECE]
    out_ref[...] = rows_ref[...].T.astype(BF16)


def response_sum(got):
    return pl.pallas_call(
        response_kernel,
        out_shape=jax.ShapeDtypeStruct((PANELS, WIDTH), BF16),
        in_specs=[pl.BlockSpec(memory_space=pltpu.VMEM)],
        out_specs=pl.BlockSpec(memory_space=pltpu.VMEM),
        scratch_shapes=[pltpu.VMEM((WIDTH, PANELS), F32)],
        compiler_params=pltpu.CompilerParams(vmem_limit_bytes=VMEM_LIMIT),
        name="response_sum",
    )(got)


def per_device(velocity, coupling, dest, cluster, near, far_v, far_u, pairs):
    messages = contributions(dest, cluster, velocity, coupling)
    messages = messages.reshape(ROWS * COLS, MESSAGE, 128)
    got = lax.all_to_all(messages, ("row", "col"), split_axis=0, concat_axis=0, tiled=True)
    own, left = cluster_sums(got, far_u[0, 0])
    pieces = gather_pieces(own)
    partial = apply_operator(pairs.reshape(-1), pieces, near[0, 0], far_v[0, 0], left)
    gathered = lax.all_to_all(partial, "col", split_axis=0, concat_axis=0, tiled=True)
    return response_sum(gathered)


def solution(mesh):
    return jax.shard_map(
        per_device,
        mesh=mesh,
        in_specs=(
            P(("row", "col"), None, None),
            P(("row", "col"), None, None, None, None),
            P(("row", "col"), None),
            P(("row", "col"), None),
            P("row", "col", None, None, None, None),
            P("row", "col", None, None, None, None),
            P("row", "col", None, None, None, None),
            P("row", "col", None),
        ),
        out_specs=P(("row", "col"), None),
        check_vma=False,
    )
```
